32 devices in a mesh: lon: 8 (over z, x), lat: 4 (over y, core).
Axes of the slice: x: 2, y: 2, z: 4, core: 2. Of those that a mesh axis runs over, the one named last changes fastest.
Arguments:
- state: float32 [2, 256, 512, 128], P(None, 'lat', 'lon'), may hold values from -6 to 6
- field_rate: float32 [2], replicated, may hold values from 0.06 to 0.24
- obs_cell: int32 [16, 32, 256], P('lat', 'lon'), may hold values from 0 to 255
- obs_value: float32 [16, 32, 256], P('lat', 'lon'), may hold values from -6 to 6
- obs_var: float32 [16, 32, 256], P('lat', 'lon'), may hold values from 0.25 to 4
- obs_count: int32 [16, 32], P('lat', 'lon'), may hold values from 128 to 256, as said below
- radius: int32 [16, 32], P('lat', 'lon'), may hold values from 6 to 13
Outputs:
- analysis: float32 [2, 256, 512, 128], P(None, 'lat', 'lon')
The draws below stay inside these ranges and needn't reach their ends.
Inputs may be any that keep to these rules, and one draw needn't show every extreme that they name: `obs_count`: every weight point has between 128 and 256 live observations, and some weight point has exactly 256.
All inputs are finite; a program needn't handle non-finite values.
Results may differ from the reference program's by a relative error of at most 0.0003.
Values sent between devices are 32-bit elements; how exact they have to be, the bound alone decides.
A program may use at most 64 MiB of HBM per device.

```python
import math
import jax
import jax.numpy as jnp
from jax import lax

FIELDS = 2
ENSEMBLE_SIZE = 128
SPACING = 16
SUBSTEPS = 4
NS_ITERS = 6
OBS_PT = 256
WEIGHT_LAT_COUNT = 16
WEIGHT_LON_COUNT = 32
NLAT = 256
NLON = 512


def draw_obs_count(key, part):
    counts = jax.random.randint(key, (WEIGHT_LAT_COUNT, WEIGHT_LON_COUNT), OBS_PT // 2, OBS_PT + 1)
    chosen = jax.random.randint(jax.random.fold_in(key, 7), (), 0, WEIGHT_LAT_COUNT * WEIGHT_LON_COUNT)
    flattened = jnp.where(jnp.arange(WEIGHT_LAT_COUNT * WEIGHT_LON_COUNT) == chosen, OBS_PT, counts.reshape(-1))
    return flattened.reshape(WEIGHT_LAT_COUNT, WEIGHT_LON_COUNT).astype(jnp.int32)


def plant(drawn, rng, least, top_value):
    place = [jax.random.randint(jax.random.fold_in(rng, axis), (), 0, length) for axis, length in enumerate(drawn.shape)]
    widest = drawn.shape.index(max(drawn.shape))
    beside = place[:widest] + [(place[widest] + 1) % drawn.shape[widest]] + place[widest + 1:]
    return drawn.at[tuple(place)].set(least).at[tuple(beside)].set(top_value)


def shard_levels(rng, shape, cuts, least, largest):
    level = 1.0
    for axis_at, blocks in cuts:
        heights = jax.random.uniform(jax.random.fold_in(jax.random.fold_in(rng, 6), axis_at), (blocks,), jnp.float32, least / len(cuts), largest / len(cuts))
        level = level * jnp.repeat(jnp.exp(heights), shape[axis_at] // blocks).reshape((-1,) + (1,) * (len(shape) - 1 - axis_at))
    return level


def bell_draw(stream_key, shape, spread, bound, cuts=(), held_as=jnp.bfloat16):
    entries = jax.random.normal(stream_key, shape, jnp.float32) * spread
    if len(cuts) > 0:
        entries = shard_levels(stream_key, shape, cuts, -0.22, 0.18) * entries
    return jnp.clip(entries, min=-bound, max=bound).astype(held_as)


def setup_inputs(seed: int = 0) -> dict:
    arg_keys = jax.random.split(jax.random.key(seed), 8)
    state = bell_draw(arg_keys[0], (FIELDS, NLAT, NLON, ENSEMBLE_SIZE), 1.0, 6.0, ((1, 4), (2, 8)), jnp.float32)
    field_rate = jnp.clip(jnp.exp(jax.random.uniform(arg_keys[1], (FIELDS,), jnp.float32, math.log(0.06), math.log(0.24))), 0.06, 0.24)
    obs_cell = plant(jax.random.randint(arg_keys[2], (WEIGHT_LAT_COUNT, WEIGHT_LON_COUNT, OBS_PT), 0, SPACING * SPACING), jax.random.fold_in(arg_keys[2], 1), 0, (SPACING * SPACING) - 1).astype(jnp.int32)
    obs_value = bell_draw(arg_keys[3], (WEIGHT_LAT_COUNT, WEIGHT_LON_COUNT, OBS_PT), 1.0, 6.0, ((0, 4), (1, 8)), jnp.float32)
    obs_var = jnp.clip(jnp.exp(math.log(4.0) - 2.7725887 * jax.random.uniform(arg_keys[4], (WEIGHT_LAT_COUNT, WEIGHT_LON_COUNT, OBS_PT), jnp.float32) ** shard_levels(arg_keys[4], (WEIGHT_LAT_COUNT, WEIGHT_LON_COUNT, OBS_PT), ((0, 4), (1, 8)), -0.2, 0.2)), 0.25, 4.0)
    obs_count = draw_obs_count(jax.random.fold_in(arg_keys[7], 71), 0)
    radius = plant(jax.random.randint(arg_keys[6], (WEIGHT_LAT_COUNT, WEIGHT_LON_COUNT), 6, 14), jax.random.fold_in(arg_keys[6], 1), 6, 13).astype(jnp.int32)
    return dict(state=state, field_rate=field_rate, obs_cell=obs_cell, obs_value=obs_value, obs_var=obs_var, obs_count=obs_count, radius=radius)


def conduct(values):
    return 0.75 + 0.25 * jnp.tanh(values)

def spread_moisture(moisture_grid, diffusivity_rate):
    row_index = jnp.arange(NLAT)[:, None, None]
    for repeat in range(SUBSTEPS):
        conducted = conduct(moisture_grid)
        east_val = jnp.roll(moisture_grid, -1, axis=1)
        west_val = jnp.roll(moisture_grid, 1, axis=1)
        south_val = jnp.roll(moisture_grid, -1, axis=0)
        north_val = jnp.roll(moisture_grid, 1, axis=0)
        net_flux = 0.5 * (conducted + jnp.roll(conducted, -1, axis=1)) * (east_val - moisture_grid)
        net_flux = net_flux + 0.5 * (conducted + jnp.roll(conducted, 1, axis=1)) * (west_val - moisture_grid)
        net_flux = net_flux + jnp.where(row_index <= NLAT - 2, 0.5 * (conducted + jnp.roll(conducted, -1, axis=0)) * (south_val - moisture_grid), 0.0)
        net_flux = net_flux + jnp.where(row_index >= 1, 0.5 * (conducted + jnp.roll(conducted, 1, axis=0)) * (north_val - moisture_grid), 0.0)
        moisture_grid = moisture_grid + diffusivity_rate * net_flux
    return moisture_grid

def point_weights(observed, located, obs_values, variances, live_count, reach):
    obs_mean = lax.optimization_barrier(jnp.mean(observed, axis=1, keepdims=True))
    member_departure = observed - obs_mean
    innovation = obs_values - obs_mean[:, 0]
    centre = 0.5 * SPACING - 0.5
    row_pos = (located // SPACING).astype(jnp.float32)
    col_pos = (located % SPACING).astype(jnp.float32)
    distance = (row_pos - centre) ** 2 + (col_pos - centre) ** 2
    reach_sq = (reach * reach).astype(jnp.float32)
    locality = jnp.maximum(1.0 - distance / reach_sq, 0.0) ** 2
    active = (jnp.arange(OBS_PT) < live_count).astype(jnp.float32)
    obs_weight = active * locality / variances
    gram_matrix = lax.dot_general(member_departure * obs_weight[:, None], member_departure, (((0,), (0,)), ((), ())), precision=lax.Precision.HIGHEST)
    identity = jnp.eye(ENSEMBLE_SIZE, dtype=jnp.float32)
    system = (ENSEMBLE_SIZE - 1.0) * identity + gram_matrix
    norm_a = jnp.sqrt(jnp.sum(system * system) + 1e-06)
    iterate = system / norm_a
    inverse = identity
    for repeat in range(NS_ITERS):
        middle = 0.5 * (3.0 * identity - jnp.dot(inverse, iterate, precision=lax.Precision.HIGHEST))
        iterate = jnp.dot(iterate, middle, precision=lax.Precision.HIGHEST)
        inverse = jnp.dot(middle, inverse, precision=lax.Precision.HIGHEST)
    forcing = jnp.dot(obs_weight * innovation, member_departure, precision=lax.Precision.HIGHEST)
    mean_weight = jnp.dot(inverse, jnp.dot(inverse, forcing, precision=lax.Precision.HIGHEST), precision=lax.Precision.HIGHEST) / norm_a
    return (ENSEMBLE_SIZE - 1.0) ** 0.5 / jnp.sqrt(norm_a) * inverse + mean_weight[:, None]

def take_rows(table, located):
    return jnp.take(table, located, axis=0)

def shares():
    offset_frac = (jnp.arange(SPACING, dtype=jnp.float32) + 0.5 - 0.5 * SPACING) / SPACING
    return (1.0 - jnp.abs(offset_frac), jnp.abs(offset_frac))

def reference(state, field_rate, obs_cell, obs_value, obs_var, obs_count, radius):
    points = WEIGHT_LAT_COUNT * WEIGHT_LON_COUNT
    first_field = spread_moisture(state[0], field_rate[0])
    tiled = first_field.reshape(WEIGHT_LAT_COUNT, SPACING, WEIGHT_LON_COUNT, SPACING, ENSEMBLE_SIZE).transpose(0, 2, 1, 3, 4).reshape(points, SPACING * SPACING, ENSEMBLE_SIZE)
    located = obs_cell.reshape(points, OBS_PT)
    observed = jax.vmap(take_rows)(tiled, located)
    weights = jax.vmap(point_weights)(observed, located, obs_value.reshape(points, OBS_PT), obs_var.reshape(points, OBS_PT), obs_count.reshape(points), radius.reshape(points))
    weights = weights.reshape(WEIGHT_LAT_COUNT, WEIGHT_LON_COUNT, ENSEMBLE_SIZE, ENSEMBLE_SIZE)
    extended = jnp.concatenate([weights[:, -1:], weights, weights[:, :1]], axis=1)
    extended = jnp.concatenate([extended[:1], extended, extended[-1:]], axis=0)
    near_share, far_share = shares()
    halved_cell_count = SPACING // 2

    def analyse(pair):
        moisture_grid, diffusivity_rate = pair
        predicted_state = spread_moisture(moisture_grid, diffusivity_rate)
        members_average = lax.optimization_barrier(jnp.mean(predicted_state, axis=2, keepdims=True))
        member_departure = (predicted_state - members_average).reshape(WEIGHT_LAT_COUNT, 2, halved_cell_count, WEIGHT_LON_COUNT, 2, halved_cell_count, ENSEMBLE_SIZE)
        lat_parts = []
        for lat_half in range(2):
            lon_parts = []
            lat_step = -1 if lat_half == 0 else 1
            near_rows = near_share[lat_half * halved_cell_count:(lat_half + 1) * halved_cell_count][None, :, None, None, None]
            far_rows = far_share[lat_half * halved_cell_count:(lat_half + 1) * halved_cell_count][None, :, None, None, None]
            for lon_half in range(2):
                lon_step = -1 if lon_half == 0 else 1
                near_cols = near_share[lon_half * halved_cell_count:(lon_half + 1) * halved_cell_count][None, None, None, :, None]
                far_cols = far_share[lon_half * halved_cell_count:(lon_half + 1) * halved_cell_count][None, None, None, :, None]
                quarter = member_departure[:, lat_half, :, :, lon_half]

                def moved(shift_lat, shift_lon):
                    chosen = extended[1 + shift_lat:1 + shift_lat + WEIGHT_LAT_COUNT, 1 + shift_lon:1 + shift_lon + WEIGHT_LON_COUNT]
                    return jnp.einsum('aibjm,abmn->aibjn', quarter, chosen, precision=lax.Precision.HIGHEST)
                summed = near_rows * near_cols * moved(0, 0)
                summed = summed + far_rows * near_cols * moved(lat_step, 0)
                summed = summed + near_rows * far_cols * moved(0, lon_step)
                summed = summed + far_rows * far_cols * moved(lat_step, lon_step)
                lon_parts.append(summed)
            lat_parts.append(jnp.concatenate(lon_parts, axis=3))
        summed_all = jnp.concatenate(lat_parts, axis=1).reshape(NLAT, NLON, ENSEMBLE_SIZE)
        return members_average + summed_all
    return lax.map(analyse, (state, field_rate))
```

```python
import jax
import jax.numpy as jnp
from jax import lax
from jax.experimental import pallas as pl
from jax.experimental.pallas import tpu as pltpu
from jax.sharding import PartitionSpec as P

SPACING = 16
SUBSTEPS = 4
NS_ITERS = 6
HALF = SPACING // 2
VMEM_BYTES = 50 * 1024 * 1024
F32 = jnp.float32
BF16 = jnp.bfloat16


def split(x):
    high = x.astype(BF16)
    return high, (x - high.astype(F32)).astype(BF16)


def product(left, right):
    n = right[0].shape[1]
    row = jnp.concatenate(right, axis=1)
    both = jnp.dot(
        jnp.concatenate(left, axis=1),
        jnp.concatenate([row, row], axis=0),
        preferred_element_type=F32,
    )
    return both[:, :n] + both[:, n:]


def diffuse(ext, out, field, rate):
    rows, cols = ext.shape[0], ext.shape[1]
    own = out.shape[2]
    scale = 0.125 * rate

    def conductance(u):
        return scale * (3.0 + jnp.tanh(u))

    for step in range(SUBSTEPS):
        first, last = step + 1, rows - 1 - step
        above, u = ext[step], ext[first]
        h_above, h = conductance(above), conductance(u)
        north = (h_above + h) * (u - above)

        def body(r, carry):
            u, h, north = carry
            below = ext[r + 1]
            h_below = conductance(below)
            south = (h + h_below) * (below - u)
            east = (h + pltpu.roll(h, cols - 1, 0)) * (pltpu.roll(u, cols - 1, 0) - u)
            new = u + ((south - north) + (east - pltpu.roll(east, 1, 0)))
            if step == SUBSTEPS - 1:
                out[field, r - SUBSTEPS] = new[:own]
            else:
                ext[r] = new
            return below, h_below, south

        lax.fori_loop(first, last, body, (u, h, north), unroll=2)


def row_weights(a, forecast, count, radius, obs_cell, obs_value, obs_var, weights):
    points = obs_cell.shape[1]
    slots = obs_cell.shape[2]
    members = forecast.shape[3]
    cells = SPACING * SPACING
    which = lax.broadcasted_iota(jnp.int32, (cells, slots), 0)
    place = lax.broadcasted_iota(jnp.int32, (cells, members), 0)
    centre = 0.5 * SPACING - 0.5
    distance = ((place // SPACING).astype(F32) - centre) ** 2 + (
        (place % SPACING).astype(F32) - centre
    ) ** 2
    slot = lax.broadcasted_iota(jnp.int32, (1, slots), 1)
    identity = (
        lax.broadcasted_iota(jnp.int32, (members, members), 0)
        == lax.broadcasted_iota(jnp.int32, (members, members), 1)
    ).astype(F32)
    ids, vals, vars_ = obs_cell[a], obs_value[a], obs_var[a]
    states = []
    for b in range(points):
        chosen = (which == ids[b : b + 1]).astype(F32).astype(BF16)
        weight = jnp.where(slot < count[a, b], 1.0 / vars_[b : b + 1], 0.0)
        valued = weight * vals[b : b + 1]
        both = jnp.concatenate(
            [
                jnp.broadcast_to(weight, (members, slots)),
                jnp.broadcast_to(valued, (members, slots)),
            ],
            axis=0,
        )
        sums = sum(
            lax.dot_general(
                chosen, part, (((1,), (1,)), ((), ())), preferred_element_type=F32
            )
            for part in split(both)
        )
        reach = radius[a, b]
        reach_sq = jnp.full((cells, members), reach * reach, jnp.int32).astype(F32)
        locality = jnp.maximum(1.0 - distance / reach_sq, 0.0) ** 2
        weight_sum = sums[:, :members] * locality
        value_sum = sums[:, members:] * locality
        tile = forecast[
            0, pl.ds(a * SPACING, SPACING), b * SPACING : (b + 1) * SPACING, :
        ].reshape(cells, members)
        average = jnp.mean(tile, axis=1, keepdims=True)
        departure = tile - average
        scaled = split(weight_sum * departure)
        forced = split(value_sum - average * weight_sum)
        quads = lax.dot_general(
            jnp.concatenate(split(departure), axis=1),
            jnp.concatenate(scaled + forced, axis=1),
            (((0,), (0,)), ((), ())),
            preferred_element_type=F32,
        )
        quads = quads[:members] + quads[members:]
        gram = quads[:, :members] + quads[:, members : 2 * members]
        forcing = quads[:, 2 * members : 3 * members] + quads[:, 3 * members :]
        system = (members - 1.0) * identity + gram
        norm = jnp.sqrt(jnp.sum(system * system, keepdims=True) + 1e-06)
        states.append((system / norm, forcing, norm))
    iterates = [split(s[0]) for s in states]
    middles = [split(1.5 * identity - 0.5 * s[0]) for s in states]
    iterates = [split(product(x, m)) for x, m in zip(iterates, middles)]
    inverses = middles
    for repeat in range(1, NS_ITERS):
        middles = [
            split(1.5 * identity - 0.5 * product(z, y))
            for z, y in zip(inverses, iterates)
        ]
        if repeat < NS_ITERS - 1:
            iterates = [split(product(y, m)) for y, m in zip(iterates, middles)]
        raw = [product(m, z) for m, z in zip(middles, inverses)]
        inverses = [split(z) for z in raw]
    for b in range(points):
        forcing, norm = states[b][1], states[b][2]
        pulled = product(inverses[b], split(product(inverses[b], split(forcing))))
        weights[a, b] = (members - 1.0) ** 0.5 / jnp.sqrt(norm) * raw[b] + pulled / norm


def forecast_kernel(
    rate, count, radius, state, sides, north, south, obs_cell, obs_value, obs_var,
    forecast, weights, ext,
):
    fields, height, width = state.shape[0], state.shape[1], state.shape[2]
    for field in range(fields):
        ext[:SUBSTEPS] = north[field]
        ext[SUBSTEPS : SUBSTEPS + height, :width] = state[field]
        ext[SUBSTEPS : SUBSTEPS + height, width:] = sides[field]
        ext[SUBSTEPS + height :] = south[field]
        diffuse(ext, forecast, field, rate[field])

    @pl.loop(0, obs_cell.shape[0])
    def _(a):
        row_weights(a, forecast, count, radius, obs_cell, obs_value, obs_var, weights)


def analysis_kernel(forecast, weights, out):
    fields, height, width, members = forecast.shape
    lat_points, lon_points = height // SPACING, width // SPACING

    def region(i, j, row, col, rows, cols, row_shift, col_shift):
        high, low = [], []
        for di, dj in ((0, 0), (0, 1), (1, 0), (1, 1)):
            h, l = split(weights[i + di, j + dj])
            high.append(h)
            low.append(l)
        high = jnp.concatenate(high, axis=1)
        low = jnp.concatenate(low, axis=1)
        right = jnp.concatenate([high, high, low, low], axis=0)
        chunk = rows // 2
        for field in range(fields):
            for part in range(2):
                start = row + part * chunk
                cells = forecast[field, pl.ds(start, chunk), pl.ds(col, cols), :]
                average = jnp.mean(cells, axis=2, keepdims=True)
                left = split((cells - average).reshape(chunk * cols, members))
                moved = jnp.dot(
                    jnp.concatenate(left + left, axis=1), right, preferred_element_type=F32
                )
                moved = [
                    moved[:, k * members : (k + 1) * members].reshape(chunk, cols, members)
                    for k in range(4)
                ]
                shape = (chunk, cols, members)
                along = lax.broadcasted_iota(jnp.int32, shape, 0) + (row_shift + part * chunk)
                across = lax.broadcasted_iota(jnp.int32, shape, 1) + col_shift
                down = (along.astype(F32) + 0.5) * (1.0 / SPACING)
                east = (across.astype(F32) + 0.5) * (1.0 / SPACING)
                upper = (1.0 - east) * moved[0] + east * moved[1]
                lower = (1.0 - east) * moved[2] + east * moved[3]
                out[field, pl.ds(start, chunk), pl.ds(col, cols), :] = average + (
                    (1.0 - down) * upper + down * lower
                )

    inner_lat, inner_lon = lat_points - 1, lon_points - 1

    @pl.loop(0, inner_lat)
    def _(i):
        row = pl.multiple_of(HALF + i * SPACING, HALF)

        @pl.loop(0, inner_lon)
        def _(j):
            col = pl.multiple_of(HALF + j * SPACING, HALF)
            region(i + 1, j + 1, row, col, SPACING, SPACING, 0, 0)

        region(i + 1, 0, row, 0, SPACING, HALF, 0, HALF)
        region(i + 1, lon_points, row, width - HALF, SPACING, HALF, 0, 0)

    @pl.loop(0, inner_lon)
    def _(j):
        col = pl.multiple_of(HALF + j * SPACING, HALF)
        region(0, j + 1, 0, col, HALF, SPACING, HALF, 0)
        region(lat_points, j + 1, height - HALF, col, HALF, SPACING, 0, 0)

    for i, row, row_shift in ((0, 0, HALF), (lat_points, height - HALF, 0)):
        for j, col, col_shift in ((0, 0, HALF), (lon_points, width - HALF, 0)):
            region(i, j, row, col, HALF, HALF, row_shift, col_shift)


def passed(x, axis, step, wrap):
    size = lax.axis_size(axis)
    pairs = [(i, (i + step) % size) for i in range(size) if wrap or 0 <= i + step < size]
    return lax.ppermute(x, axis, pairs)


def local(state, field_rate, obs_cell, obs_value, obs_var, obs_count, radius):
    fields, height, width, members = state.shape
    lat_points, lon_points = obs_cell.shape[0], obs_cell.shape[1]
    lat_index = lax.axis_index("lat")
    lat_bands = lax.axis_size("lat")
    g = SUBSTEPS
    east = passed(state[:, :, :g], "lon", -1, True)
    west = passed(state[:, :, width - g :], "lon", 1, True)
    sides = jnp.concatenate([east, west], axis=2)

    def whole_rows(part):
        return jnp.concatenate([state[:, part], sides[:, part]], axis=2)

    top, bottom = whole_rows(slice(0, g)), whole_rows(slice(height - g, height))
    north = passed(bottom, "lat", 1, False)
    south = passed(top, "lat", -1, False)
    north = jnp.where(lat_index == 0, top[:, ::-1], north)
    south = jnp.where(lat_index == lat_bands - 1, bottom[:, ::-1], south)
    vmem = pl.BlockSpec(memory_space=pltpu.VMEM)
    smem = pl.BlockSpec(memory_space=pltpu.SMEM)
    forecast, weights = pl.pallas_call(
        forecast_kernel,
        out_shape=(
            jax.ShapeDtypeStruct(state.shape, F32),
            jax.ShapeDtypeStruct((lat_points, lon_points, members, members), F32),
        ),
        in_specs=[smem] * 3 + [vmem] * 7,
        out_specs=(vmem, vmem),
        scratch_shapes=[pltpu.VMEM((height + 2 * g, width + 2 * g, members), F32)],
        compiler_params=pltpu.CompilerParams(vmem_limit_bytes=VMEM_BYTES),
    )(field_rate, obs_count, radius, state, sides, north, south, obs_cell, obs_value, obs_var)

    before = passed(weights[:, -1:], "lon", 1, True)
    after = passed(weights[:, :1], "lon", -1, True)
    weights = jnp.concatenate([before, weights, after], axis=1)
    first, last = weights[:1], weights[-1:]
    above = jnp.where(lat_index == 0, first, passed(last, "lat", 1, False))
    below = jnp.where(lat_index == lat_bands - 1, last, passed(first, "lat", -1, False))
    weights = jnp.concatenate([above, weights, below], axis=0)
    return pl.pallas_call(
        analysis_kernel,
        out_shape=jax.ShapeDtypeStruct(state.shape, F32),
        in_specs=[vmem] * 2,
        out_specs=vmem,
        compiler_params=pltpu.CompilerParams(vmem_limit_bytes=VMEM_BYTES),
    )(forecast, weights)


def solution(mesh):
    in_specs = (
        P(None, "lat", "lon", None),
        P(),
        P("lat", "lon", None),
        P("lat", "lon", None),
        P("lat", "lon", None),
        P("lat", "lon"),
        P("lat", "lon"),
    )
    out_specs = P(None, "lat", "lon", None)
    return jax.shard_map(local, mesh=mesh, in_specs=in_specs, out_specs=out_specs, check_vma=False)
```

```python
import jax
import jax.numpy as jnp
from jax import lax
from jax.experimental import pallas as pl
from jax.experimental.pallas import tpu as pltpu
from jax.sharding import PartitionSpec as P

SPACING = 16
SUBSTEPS = 4
NS_ITERS = 6
HALF = SPACING // 2
VMEM_BYTES = 50 * 1024 * 1024
F32 = jnp.float32
BF16 = jnp.bfloat16


def split(x):
    high = x.astype(BF16)
    return high, (x - high.astype(F32)).astype(BF16)


def product(left, right):
    n = right[0].shape[1]
    row = jnp.concatenate(right, axis=1)
    both = jnp.dot(
        jnp.concatenate(left, axis=1),
        jnp.concatenate([row, row], axis=0),
        preferred_element_type=F32,
    )
    return both[:, :n] + both[:, n:]


def substep(step, field, rate, ext, out):
    rows, cols = ext.shape[1], ext.shape[2]
    own = out.shape[2]
    scale = 0.125 * rate
    first, last = step + 1, rows - 1 - step

    def conductance(u):
        return scale * (3.0 + jnp.tanh(u))

    def body(r, carry):
        u, h, north = carry
        below = ext[field, r + 1]
        h_below = conductance(below)
        south = (h + h_below) * (below - u)
        east = (h + pltpu.roll(h, cols - 1, 0)) * (pltpu.roll(u, cols - 1, 0) - u)
        new = u + ((south - north) + (east - pltpu.roll(east, 1, 0)))
        if step == SUBSTEPS - 1:
            out[field, r - SUBSTEPS] = new[:own]
        else:
            ext[field, r] = new
        return below, h_below, south

    above, u = ext[field, step], ext[field, first]
    h_above, h = conductance(above), conductance(u)
    lax.fori_loop(first, last, body, (u, h, (h_above + h) * (u - above)), unroll=2)


def point_sums(a, b, count, radius, obs_cell, obs_value, obs_var, sums):
    slots = obs_cell.shape[2]
    cells, members = sums.shape[2], sums.shape[3] // 2
    which = lax.broadcasted_iota(jnp.int32, (cells, slots), 0)
    place = lax.broadcasted_iota(jnp.int32, (cells, members), 0)
    centre = 0.5 * SPACING - 0.5
    distance = ((place // SPACING).astype(F32) - centre) ** 2 + (
        (place % SPACING).astype(F32) - centre
    ) ** 2
    slot = lax.broadcasted_iota(jnp.int32, (1, slots), 1)
    one = pl.ds(b, 1)
    chosen = (which == obs_cell[a, one]).astype(F32).astype(BF16)
    weight = jnp.where(slot < count[a, b], 1.0 / obs_var[a, one], 0.0)
    valued = weight * obs_value[a, one]
    both = jnp.concatenate(
        [
            jnp.broadcast_to(weight, (members, slots)),
            jnp.broadcast_to(valued, (members, slots)),
        ],
        axis=0,
    )
    found = sum(
        lax.dot_general(chosen, part, (((1,), (1,)), ((), ())), preferred_element_type=F32)
        for part in split(both)
    )
    reach = radius[a, b]
    reach_sq = jnp.full((cells, members), reach * reach, jnp.int32).astype(F32)
    locality = jnp.maximum(1.0 - distance / reach_sq, 0.0) ** 2
    sums[a, b, :, :members] = found[:, :members] * locality
    sums[a, b, :, members:] = found[:, members:] * locality


def column_weights(b, forecast, sums, weights):
    lat_points, cells = sums.shape[0], sums.shape[2]
    members = forecast.shape[3]
    col = pl.multiple_of(b * SPACING, SPACING)
    identity = (
        lax.broadcasted_iota(jnp.int32, (members, members), 0)
        == lax.broadcasted_iota(jnp.int32, (members, members), 1)
    ).astype(F32)
    states = []
    for a in range(lat_points):
        weight_sum = sums[a, b, :, :members]
        value_sum = sums[a, b, :, members:]
        tile = forecast[0, a * SPACING : (a + 1) * SPACING, pl.ds(col, SPACING), :]
        tile = tile.reshape(cells, members)
        average = jnp.mean(tile, axis=1, keepdims=True)
        departure = tile - average
        scaled = split(weight_sum * departure)
        forced = split(value_sum - average * weight_sum)
        quads = lax.dot_general(
            jnp.concatenate(split(departure), axis=1),
            jnp.concatenate(scaled + forced, axis=1),
            (((0,), (0,)), ((), ())),
            preferred_element_type=F32,
        )
        quads = quads[:members] + quads[members:]
        gram = quads[:, :members] + quads[:, members : 2 * members]
        forcing = quads[:, 2 * members : 3 * members] + quads[:, 3 * members :]
        system = (members - 1.0) * identity + gram
        norm = jnp.sqrt(jnp.sum(system * system, keepdims=True) + 1e-06)
        states.append((system / norm, forcing, norm))
    iterates = [split(s[0]) for s in states]
    middles = [split(1.5 * identity - 0.5 * s[0]) for s in states]
    iterates = [split(product(x, m)) for x, m in zip(iterates, middles)]
    inverses = middles
    for repeat in range(1, NS_ITERS):
        middles = [
            split(1.5 * identity - 0.5 * product(z, y)) for z, y in zip(inverses, iterates)
        ]
        if repeat < NS_ITERS - 1:
            iterates = [split(product(y, m)) for y, m in zip(iterates, middles)]
        raw = [product(m, z) for m, z in zip(middles, inverses)]
        inverses = [split(z) for z in raw]
    for a in range(lat_points):
        forcing, norm = states[a][1], states[a][2]
        pulled = product(inverses[a], split(product(inverses[a], split(forcing))))
        weights[a + 1, b + 1] = (
            (members - 1.0) ** 0.5 / jnp.sqrt(norm) * raw[a] + pulled / norm
        )


def forecast_kernel(
    rate, count, radius, obs_cell, obs_value, obs_var, state,
    forecast_out, weights,
    ext, packed, got, sums, forecast, load_sem, store_sem, send_sem, recv_sem,
):
    fields, height, width = state.shape[0], state.shape[1], state.shape[2]
    lat_points, lon_points = sums.shape[0], sums.shape[1]
    g = SUBSTEPS
    end = g + height
    half = height // 2
    lon, lat = lax.axis_index("lon"), lax.axis_index("lat")
    lon_size, lat_size = lax.axis_size("lon"), lax.axis_size("lat")
    has_north, has_south = lat > 0, lat < lat_size - 1
    to_east = {"lon": lax.rem(lon + 1, lon_size)}
    to_west = {"lon": lax.rem(lon + lon_size - 1, lon_size)}
    to_north = {"lat": lax.rem(lat + lat_size - 1, lat_size)}
    to_south = {"lat": lax.rem(lat + 1, lat_size)}
    mesh_ids = pl.DeviceIdType.MESH

    barrier = pltpu.get_barrier_semaphore()
    pl.semaphore_signal(barrier, inc=1, device_id=to_east, device_id_type=mesh_ids)
    pl.semaphore_signal(barrier, inc=1, device_id=to_west, device_id_type=mesh_ids)

    @pl.when(has_north)
    def _():
        pl.semaphore_signal(barrier, inc=1, device_id=to_north, device_id_type=mesh_ids)

    @pl.when(has_south)
    def _():
        pl.semaphore_signal(barrier, inc=1, device_id=to_south, device_id_type=mesh_ids)

    loads = [
        pltpu.make_async_copy(state.at[f], ext.at[f, g:end, :width], load_sem.at[f])
        for f in range(fields)
    ]
    for load in loads:
        load.start()
    north_peers = lax.div(lat + lat_size - 1, lat_size)
    south_peers = lax.div(2 * lat_size - 2 - lat, lat_size)
    pl.semaphore_wait(barrier, 2 + north_peers + south_peers)

    def remote(k, src, dst, target):
        return pltpu.make_async_remote_copy(
            src_ref=src, dst_ref=dst, send_sem=send_sem.at[k], recv_sem=recv_sem.at[k],
            device_id=target, device_id_type=mesh_ids,
        )

    def start_lat(north, south):
        @pl.when(has_north)
        def _():
            for copy in north:
                copy.start()

        @pl.when(has_south)
        def _():
            for copy in south:
                copy.start()

    def wait_lat(north, south):
        @pl.when(has_north)
        def _():
            for copy in north:
                copy.wait_send()
            for copy in south:
                copy.wait_recv()

        @pl.when(has_south)
        def _():
            for copy in south:
                copy.wait_send()
            for copy in north:
                copy.wait_recv()

    eastward, westward, northward, southward, corner_n, corner_s = [], [], [], [], [], []
    for f in range(fields):
        k = 6 * f
        eastward.append(remote(k, packed.at[f, 1], got.at[f, 1], to_east))
        westward.append(remote(k + 1, packed.at[f, 0], got.at[f, 0], to_west))
        northward.append(remote(k + 2, state.at[f, :g], ext.at[f, end:, :width], to_north))
        southward.append(
            remote(k + 3, state.at[f, height - g :], ext.at[f, :g, :width], to_south)
        )
        corner_n.append(
            remote(k + 4, ext.at[f, g : 2 * g, width:], ext.at[f, end:, width:], to_north)
        )
        corner_s.append(
            remote(k + 5, ext.at[f, height:end, width:], ext.at[f, :g, width:], to_south)
        )

    def send_ghosts(f):
        for side, cols, part in (
            (1, slice(width - 2 * g, width), slice(g, None)),
            (0, slice(0, 2 * g), slice(0, g)),
        ):
            upper = ext[f, g : g + half, cols][:, part]
            lower = ext[f, g + half : end, cols][:, part]
            packed[f, side] = jnp.concatenate([upper, lower], axis=1)
            (westward, eastward)[side][f].start()
        start_lat([northward[f]], [southward[f]])

    def place_sides(f):
        eastward[f].wait()
        westward[f].wait()
        east, west = got[f, 0], got[f, 1]
        ext[f, g : g + half, width:] = jnp.concatenate([east[:, :g], west[:, :g]], axis=1)
        ext[f, g + half : end, width:] = jnp.concatenate([east[:, g:], west[:, g:]], axis=1)
        start_lat([corner_n[f]], [corner_s[f]])

    def finish_ghosts(f):
        wait_lat([northward[f], corner_n[f]], [southward[f], corner_s[f]])

        @pl.when(jnp.logical_not(has_north))
        def _():
            for r in range(g):
                ext[f, r] = ext[f, 2 * g - 1 - r]

        @pl.when(jnp.logical_not(has_south))
        def _():
            for r in range(g):
                ext[f, end + r] = ext[f, end - 1 - r]

    for f in range(fields):
        loads[f].wait()
        if f == 0:
            send_ghosts(f)

    @pl.loop(0, lat_points)
    def _(a):
        @pl.loop(0, lon_points)
        def _(b):
            point_sums(a, b, count, radius, obs_cell, obs_value, obs_var, sums)

    stores = [
        pltpu.make_async_copy(forecast.at[f], forecast_out.at[f], store_sem.at[f])
        for f in range(fields)
    ]
    place_sides(0)
    for f in range(1, fields):
        send_ghosts(f)
    finish_ghosts(0)
    for step in range(SUBSTEPS):
        substep(step, 0, rate[0], ext, forecast)
    stores[0].start()

    k = 6 * fields
    lat_rows, lon_cols = pl.ds(1, lat_points), pl.ds(1, lon_points)
    w_east = remote(k, weights.at[lat_rows, lon_points], weights.at[lat_rows, 0], to_east)
    w_west = remote(
        k + 1, weights.at[lat_rows, 1], weights.at[lat_rows, lon_points + 1], to_west
    )
    w_north = [remote(k + 2, weights.at[1, lon_cols], weights.at[lat_points + 1, lon_cols], to_north)]
    w_south = [remote(k + 3, weights.at[lat_points, lon_cols], weights.at[0, lon_cols], to_south)]
    c_north, c_south = [], []
    for n, b in enumerate((0, lon_points + 1)):
        c_north.append(
            remote(k + 4 + n, weights.at[1, b], weights.at[lat_points + 1, b], to_north)
        )
        c_south.append(remote(k + 6 + n, weights.at[lat_points, b], weights.at[0, b], to_south))

    @pl.loop(0, 2)
    def _(n):
        column_weights(n * (lon_points - 1), forecast, sums, weights)

    w_east.start()
    w_west.start()
    for f in range(1, fields):
        place_sides(f)

    @pl.loop(1, lon_points - 1)
    def _(b):
        column_weights(b, forecast, sums, weights)

    start_lat(w_north, w_south)
    for f in range(1, fields):
        finish_ghosts(f)
        for step in range(SUBSTEPS):
            substep(step, f, rate[f], ext, forecast)
            if f == fields - 1 and step == SUBSTEPS - 2:
                w_east.wait()
                w_west.wait()
                start_lat(c_north, c_south)
        stores[f].start()
    wait_lat(w_north + c_north, w_south + c_south)

    @pl.when(jnp.logical_not(has_north))
    def _():
        weights[0] = weights[1]

    @pl.when(jnp.logical_not(has_south))
    def _():
        weights[lat_points + 1] = weights[lat_points]

    for store in stores:
        store.wait()


def analysis_kernel(forecast, weights, out):
    fields, height, width, members = forecast.shape
    lat_points, lon_points = height // SPACING, width // SPACING

    def region(i, j, row, col, rows, cols, row_shift, col_shift):
        high, low = [], []
        for di, dj in ((0, 0), (0, 1), (1, 0), (1, 1)):
            h, l = split(weights[i + di, j + dj])
            high.append(h)
            low.append(l)
        high = jnp.concatenate(high, axis=1)
        low = jnp.concatenate(low, axis=1)
        right = jnp.concatenate([high, high, low, low], axis=0)
        chunk = rows // 2
        for field in range(fields):
            for part in range(2):
                start = row + part * chunk
                cells = forecast[field, pl.ds(start, chunk), pl.ds(col, cols), :]
                average = jnp.mean(cells, axis=2, keepdims=True)
                left = split((cells - average).reshape(chunk * cols, members))
                moved = jnp.dot(
                    jnp.concatenate(left + left, axis=1), right, preferred_element_type=F32
                )
                moved = [
                    moved[:, k * members : (k + 1) * members].reshape(chunk, cols, members)
                    for k in range(4)
                ]
                shape = (chunk, cols, members)
                along = lax.broadcasted_iota(jnp.int32, shape, 0) + (row_shift + part * chunk)
                across = lax.broadcasted_iota(jnp.int32, shape, 1) + col_shift
                down = (along.astype(F32) + 0.5) * (1.0 / SPACING)
                east = (across.astype(F32) + 0.5) * (1.0 / SPACING)
                upper = (1.0 - east) * moved[0] + east * moved[1]
                lower = (1.0 - east) * moved[2] + east * moved[3]
                out[field, pl.ds(start, chunk), pl.ds(col, cols), :] = average + (
                    (1.0 - down) * upper + down * lower
                )

    inner_lat, inner_lon = lat_points - 1, lon_points - 1

    @pl.loop(0, inner_lat)
    def _(i):
        row = pl.multiple_of(HALF + i * SPACING, HALF)

        @pl.loop(0, inner_lon)
        def _(j):
            col = pl.multiple_of(HALF + j * SPACING, HALF)
            region(i + 1, j + 1, row, col, SPACING, SPACING, 0, 0)

        region(i + 1, 0, row, 0, SPACING, HALF, 0, HALF)
        region(i + 1, lon_points, row, width - HALF, SPACING, HALF, 0, 0)

    @pl.loop(0, inner_lon)
    def _(j):
        col = pl.multiple_of(HALF + j * SPACING, HALF)
        region(0, j + 1, 0, col, HALF, SPACING, HALF, 0)
        region(lat_points, j + 1, height - HALF, col, HALF, SPACING, 0, 0)

    for i, row, row_shift in ((0, 0, HALF), (lat_points, height - HALF, 0)):
        for j, col, col_shift in ((0, 0, HALF), (lon_points, width - HALF, 0)):
            region(i, j, row, col, HALF, HALF, row_shift, col_shift)


def local(state, field_rate, obs_cell, obs_value, obs_var, obs_count, radius):
    fields, height, width, members = state.shape
    lat_points, lon_points = obs_cell.shape[0], obs_cell.shape[1]
    g = SUBSTEPS
    vmem = pl.BlockSpec(memory_space=pltpu.VMEM)
    smem = pl.BlockSpec(memory_space=pltpu.SMEM)
    anywhere = pl.BlockSpec(memory_space=pl.ANY)
    sides = pltpu.VMEM((fields, 2, height // 2, 2 * g, members), F32)
    copies = 6 * fields + 8
    forecast, weights = pl.pallas_call(
        forecast_kernel,
        out_shape=(
            jax.ShapeDtypeStruct(state.shape, F32),
            jax.ShapeDtypeStruct((lat_points + 2, lon_points + 2, members, members), F32),
        ),
        in_specs=[smem] * 3 + [vmem] * 3 + [anywhere],
        out_specs=(anywhere, vmem),
        scratch_shapes=[
            pltpu.VMEM((fields, height + 2 * g, width + 2 * g, members), F32),
            sides,
            sides,
            pltpu.VMEM((lat_points, lon_points, SPACING * SPACING, 2 * members), F32),
            pltpu.VMEM(state.shape, F32),
            pltpu.SemaphoreType.DMA((fields,)),
            pltpu.SemaphoreType.DMA((fields,)),
            pltpu.SemaphoreType.DMA((copies,)),
            pltpu.SemaphoreType.DMA((copies,)),
        ],
        compiler_params=pltpu.CompilerParams(
            vmem_limit_bytes=VMEM_BYTES, collective_id=0, has_side_effects=True
        ),
    )(field_rate, obs_count, radius, obs_cell, obs_value, obs_var, state)
    field_block = pl.BlockSpec((1, height, width, members), lambda f: (f, 0, 0, 0))
    return pl.pallas_call(
        analysis_kernel,
        grid=(fields,),
        out_shape=jax.ShapeDtypeStruct(state.shape, F32),
        in_specs=[field_block, vmem],
        out_specs=field_block,
        compiler_params=pltpu.CompilerParams(vmem_limit_bytes=VMEM_BYTES),
    )(forecast, weights)


def solution(mesh):
    in_specs = (
        P(None, "lat", "lon", None),
        P(),
        P("lat", "lon", None),
        P("lat", "lon", None),
        P("lat", "lon", None),
        P("lat", "lon"),
        P("lat", "lon"),
    )
    out_specs = P(None, "lat", "lon", None)
    return jax.shard_map(local, mesh=mesh, in_specs=in_specs, out_specs=out_specs, check_vma=False)
```

```python
import jax
import jax.numpy as jnp
from jax import lax
from jax.experimental import pallas as pl
from jax.experimental.pallas import tpu as pltpu
from jax.sharding import PartitionSpec as P

SPACING = 16
SUBSTEPS = 4
NS_ITERS = 6
HALF = SPACING // 2
VMEM_BYTES = 50 * 1024 * 1024
F32 = jnp.float32
BF16 = jnp.bfloat16


def split(x):
    high = x.astype(BF16)
    return high, (x - high.astype(F32)).astype(BF16)


def product(left, right):
    n = right[0].shape[1]
    row = jnp.concatenate(right, axis=1)
    both = jnp.dot(
        jnp.concatenate(left, axis=1),
        jnp.concatenate([row, row], axis=0),
        preferred_element_type=F32,
    )
    return both[:, :n] + both[:, n:]


def substep(step, field, rate, ext, out):
    rows, cols = ext.shape[1], ext.shape[2]
    own = out.shape[2]
    scale = 0.125 * rate
    first, last = step + 1, rows - 1 - step

    def conductance(u):
        return scale * (3.0 + jnp.tanh(u))

    def body(r, carry):
        u, h, north = carry
        below = ext[field, r + 1]
        h_below = conductance(below)
        south = (h + h_below) * (below - u)
        east = (h + pltpu.roll(h, cols - 1, 0)) * (pltpu.roll(u, cols - 1, 0) - u)
        new = u + ((south - north) + (east - pltpu.roll(east, 1, 0)))
        if step == SUBSTEPS - 1:
            out[field, r - SUBSTEPS] = new[:own]
        else:
            ext[field, r] = new
        return below, h_below, south

    above, u = ext[field, step], ext[field, first]
    h_above, h = conductance(above), conductance(u)
    lax.fori_loop(first, last, body, (u, h, (h_above + h) * (u - above)), unroll=2)


def point_sums(a, b, count, radius, obs_cell, obs_value, obs_var, sums):
    slots = obs_cell.shape[2]
    cells, members = sums.shape[2], sums.shape[3] // 2
    which = lax.broadcasted_iota(jnp.int32, (cells, slots), 0)
    place = lax.broadcasted_iota(jnp.int32, (cells, members), 0)
    centre = 0.5 * SPACING - 0.5
    distance = ((place // SPACING).astype(F32) - centre) ** 2 + (
        (place % SPACING).astype(F32) - centre
    ) ** 2
    slot = lax.broadcasted_iota(jnp.int32, (1, slots), 1)
    one = pl.ds(b, 1)
    chosen = (which == obs_cell[a, one]).astype(F32).astype(BF16)
    weight = jnp.where(slot < count[a, b], 1.0 / obs_var[a, one], 0.0)
    valued = weight * obs_value[a, one]
    both = jnp.concatenate(
        [
            jnp.broadcast_to(weight, (members, slots)),
            jnp.broadcast_to(valued, (members, slots)),
        ],
        axis=0,
    )
    found = sum(
        lax.dot_general(chosen, part, (((1,), (1,)), ((), ())), preferred_element_type=F32)
        for part in split(both)
    )
    reach = radius[a, b]
    reach_sq = jnp.full((cells, members), reach * reach, jnp.int32).astype(F32)
    locality = jnp.maximum(1.0 - distance / reach_sq, 0.0) ** 2
    sums[a, b, :, :members] = found[:, :members] * locality
    sums[a, b, :, members:] = found[:, members:] * locality


def column_weights(columns, forecast, sums, weights):
    lat_points, cells = sums.shape[0], sums.shape[2]
    members = forecast.shape[3]
    points = [(a, b) for b in columns for a in range(lat_points)]
    identity = (
        lax.broadcasted_iota(jnp.int32, (members, members), 0)
        == lax.broadcasted_iota(jnp.int32, (members, members), 1)
    ).astype(F32)
    states = []
    for a, b in points:
        weight_sum = sums[a, b, :, :members]
        value_sum = sums[a, b, :, members:]
        tile = forecast[
            0, a * SPACING : (a + 1) * SPACING, b * SPACING : (b + 1) * SPACING, :
        ]
        tile = tile.reshape(cells, members)
        average = jnp.mean(tile, axis=1, keepdims=True)
        departure = tile - average
        scaled = split(weight_sum * departure)
        forced = split(value_sum - average * weight_sum)
        quads = lax.dot_general(
            jnp.concatenate(split(departure), axis=1),
            jnp.concatenate(scaled + forced, axis=1),
            (((0,), (0,)), ((), ())),
            preferred_element_type=F32,
        )
        quads = quads[:members] + quads[members:]
        gram = quads[:, :members] + quads[:, members : 2 * members]
        forcing = quads[:, 2 * members : 3 * members] + quads[:, 3 * members :]
        system = (members - 1.0) * identity + gram
        norm = jnp.sqrt(jnp.sum(system * system, keepdims=True) + 1e-06)
        states.append((system / norm, forcing, norm))
    iterates = [split(s[0]) for s in states]
    middles = [split(1.5 * identity - 0.5 * s[0]) for s in states]
    iterates = [split(product(x, m)) for x, m in zip(iterates, middles)]
    inverses = middles
    for repeat in range(1, NS_ITERS):
        middles = [
            split(1.5 * identity - 0.5 * product(z, y)) for z, y in zip(inverses, iterates)
        ]
        if repeat < NS_ITERS - 1:
            iterates = [split(product(y, m)) for y, m in zip(iterates, middles)]
        raw = [product(m, z) for m, z in zip(middles, inverses)]
        inverses = [split(z) for z in raw]
    for n, (a, b) in enumerate(points):
        forcing, norm = states[n][1], states[n][2]
        pulled = product(inverses[n], split(product(inverses[n], split(forcing))))
        moved = (members - 1.0) ** 0.5 / jnp.sqrt(norm) * raw[n] + pulled / norm
        weights[a + 1, b + 1] = moved + (1.0 / members - jnp.mean(moved, axis=0, keepdims=True))


def forecast_kernel(
    rate_in, count_in, radius_in, cell_in, value_in, var_in, state,
    forecast_out, weights,
    rate, count, radius, obs_cell, obs_value, obs_var,
    ext, packed, got, sums, forecast, small_sem, load_sem, store_sem, send_sem, recv_sem,
):
    fields, height, width = state.shape[0], state.shape[1], state.shape[2]
    lat_points, lon_points = sums.shape[0], sums.shape[1]
    g = SUBSTEPS
    end = g + height
    half = height // 2
    lon, lat = lax.axis_index("lon"), lax.axis_index("lat")
    lon_size, lat_size = lax.axis_size("lon"), lax.axis_size("lat")
    has_north, has_south = lat > 0, lat < lat_size - 1
    to_east = {"lon": lax.rem(lon + 1, lon_size)}
    to_west = {"lon": lax.rem(lon + lon_size - 1, lon_size)}
    to_north = {"lat": lax.rem(lat + lat_size - 1, lat_size)}
    to_south = {"lat": lax.rem(lat + 1, lat_size)}
    mesh_ids = pl.DeviceIdType.MESH

    barrier = pltpu.get_barrier_semaphore()
    pl.semaphore_signal(barrier, inc=1, device_id=to_east, device_id_type=mesh_ids)
    pl.semaphore_signal(barrier, inc=1, device_id=to_west, device_id_type=mesh_ids)

    @pl.when(has_north)
    def _():
        pl.semaphore_signal(barrier, inc=1, device_id=to_north, device_id_type=mesh_ids)

    @pl.when(has_south)
    def _():
        pl.semaphore_signal(barrier, inc=1, device_id=to_south, device_id_type=mesh_ids)

    loads = [
        pltpu.make_async_copy(state.at[f], ext.at[f, g:end, :width], load_sem.at[f])
        for f in range(fields)
    ]
    small = [
        pltpu.make_async_copy(src, dst, small_sem.at[n])
        for n, (src, dst) in enumerate(
            (
                (rate_in, rate),
                (count_in, count),
                (radius_in, radius),
                (cell_in, obs_cell),
                (value_in, obs_value),
                (var_in, obs_var),
            )
        )
    ]
    for load in loads + small:
        load.start()
    north_peers = lax.div(lat + lat_size - 1, lat_size)
    south_peers = lax.div(2 * lat_size - 2 - lat, lat_size)
    pl.semaphore_wait(barrier, 2 + north_peers + south_peers)

    def remote(k, src, dst, target):
        return pltpu.make_async_remote_copy(
            src_ref=src, dst_ref=dst, send_sem=send_sem.at[k], recv_sem=recv_sem.at[k],
            device_id=target, device_id_type=mesh_ids,
        )

    def start_lat(north, south):
        @pl.when(has_north)
        def _():
            for copy in north:
                copy.start()

        @pl.when(has_south)
        def _():
            for copy in south:
                copy.start()

    def wait_lat(north, south):
        @pl.when(has_north)
        def _():
            for copy in north:
                copy.wait_send()
            for copy in south:
                copy.wait_recv()

        @pl.when(has_south)
        def _():
            for copy in south:
                copy.wait_send()
            for copy in north:
                copy.wait_recv()

    eastward, westward, northward, southward, corner_n, corner_s = [], [], [], [], [], []
    for f in range(fields):
        k = 6 * f
        eastward.append(remote(k, packed.at[f, 1], got.at[f, 1], to_east))
        westward.append(remote(k + 1, packed.at[f, 0], got.at[f, 0], to_west))
        northward.append(remote(k + 2, state.at[f, :g], ext.at[f, end:, :width], to_north))
        southward.append(
            remote(k + 3, state.at[f, height - g :], ext.at[f, :g, :width], to_south)
        )
        corner_n.append(
            remote(k + 4, ext.at[f, g : 2 * g, width:], ext.at[f, end:, width:], to_north)
        )
        corner_s.append(
            remote(k + 5, ext.at[f, height:end, width:], ext.at[f, :g, width:], to_south)
        )

    def send_ghosts(f):
        for side, cols, part in (
            (1, slice(width - 2 * g, width), slice(g, None)),
            (0, slice(0, 2 * g), slice(0, g)),
        ):
            upper = ext[f, g : g + half, cols][:, part]
            lower = ext[f, g + half : end, cols][:, part]
            packed[f, side] = jnp.concatenate([upper, lower], axis=1)
            (westward, eastward)[side][f].start()
        start_lat([northward[f]], [southward[f]])

    def place_sides(f):
        eastward[f].wait()
        westward[f].wait()
        east, west = got[f, 0], got[f, 1]
        ext[f, g : g + half, width:] = jnp.concatenate([east[:, :g], west[:, :g]], axis=1)
        ext[f, g + half : end, width:] = jnp.concatenate([east[:, g:], west[:, g:]], axis=1)
        start_lat([corner_n[f]], [corner_s[f]])

    def finish_ghosts(f):
        wait_lat([northward[f], corner_n[f]], [southward[f], corner_s[f]])

        @pl.when(jnp.logical_not(has_north))
        def _():
            for r in range(g):
                ext[f, r] = ext[f, 2 * g - 1 - r]

        @pl.when(jnp.logical_not(has_south))
        def _():
            for r in range(g):
                ext[f, end + r] = ext[f, end - 1 - r]

    for f in range(fields):
        loads[f].wait()
        if f == 0:
            send_ghosts(f)

    for load in small:
        load.wait()

    @pl.loop(0, lat_points)
    def _(a):
        @pl.loop(0, lon_points)
        def _(b):
            point_sums(a, b, count, radius, obs_cell, obs_value, obs_var, sums)

    stores = [
        pltpu.make_async_copy(forecast.at[f], forecast_out.at[f], store_sem.at[f])
        for f in range(fields)
    ]
    place_sides(0)
    for f in range(1, fields):
        send_ghosts(f)
    finish_ghosts(0)
    for step in range(SUBSTEPS):
        substep(step, 0, rate[0], ext, forecast)
    stores[0].start()

    k = 6 * fields
    lat_rows, lon_cols = pl.ds(1, lat_points), pl.ds(1, lon_points)
    w_east = remote(k, weights.at[lat_rows, lon_points], weights.at[lat_rows, 0], to_east)
    w_west = remote(
        k + 1, weights.at[lat_rows, 1], weights.at[lat_rows, lon_points + 1], to_west
    )
    w_north = [remote(k + 2, weights.at[1, lon_cols], weights.at[lat_points + 1, lon_cols], to_north)]
    w_south = [remote(k + 3, weights.at[lat_points, lon_cols], weights.at[0, lon_cols], to_south)]
    c_north, c_south = [], []
    for n, b in enumerate((0, lon_points + 1)):
        c_north.append(
            remote(k + 4 + n, weights.at[1, b], weights.at[lat_points + 1, b], to_north)
        )
        c_south.append(remote(k + 6 + n, weights.at[lat_points, b], weights.at[0, b], to_south))

    column_weights((0, lon_points - 1), forecast, sums, weights)

    w_east.start()
    w_west.start()
    for f in range(1, fields):
        place_sides(f)

    for b in range(1, lon_points - 1, 2):
        column_weights(range(b, min(b + 2, lon_points - 1)), forecast, sums, weights)

    start_lat(w_north, w_south)
    for f in range(1, fields):
        finish_ghosts(f)
        for step in range(SUBSTEPS):
            substep(step, f, rate[f], ext, forecast)
            if f == fields - 1 and step == SUBSTEPS - 2:
                w_east.wait()
                w_west.wait()
                start_lat(c_north, c_south)
        stores[f].start()
    wait_lat(w_north + c_north, w_south + c_south)

    @pl.when(jnp.logical_not(has_north))
    def _():
        weights[0] = weights[1]

    @pl.when(jnp.logical_not(has_south))
    def _():
        weights[lat_points + 1] = weights[lat_points]

    for store in stores:
        store.wait()


def analysis_kernel(forecast, weights, out, parts):
    fields, height, width, members = forecast.shape
    lat_points, lon_points = height // SPACING, width // SPACING

    @pl.when(pl.program_id(0) == 0)
    def _():
        @pl.loop(0, lat_points + 2)
        def _(i):
            for j in range(lon_points + 2):
                parts[0, i, j], parts[1, i, j] = split(weights[i, j])

    def region(i, j, row, col, rows, cols, row_shift, col_shift):
        corners = ((0, 0), (0, 1), (1, 0), (1, 1))
        high, low = (
            jnp.concatenate([parts[n, i + di, j + dj] for di, dj in corners], axis=1)
            for n in range(2)
        )
        right = jnp.concatenate([high, high, low], axis=0)
        chunk = rows // 2
        for field in range(fields):
            for part in range(2):
                start = row + part * chunk
                cells = forecast[field, pl.ds(start, chunk), pl.ds(col, cols), :]
                left = split(cells.reshape(chunk * cols, members))
                moved = jnp.dot(
                    jnp.concatenate(left + left[:1], axis=1), right, preferred_element_type=F32
                )
                moved = [
                    moved[:, k * members : (k + 1) * members].reshape(chunk, cols, members)
                    for k in range(4)
                ]
                shape = (chunk, cols, members)
                along = lax.broadcasted_iota(jnp.int32, shape, 0) + (row_shift + part * chunk)
                across = lax.broadcasted_iota(jnp.int32, shape, 1) + col_shift
                down = (along.astype(F32) + 0.5) * (1.0 / SPACING)
                east = (across.astype(F32) + 0.5) * (1.0 / SPACING)
                upper = (1.0 - east) * moved[0] + east * moved[1]
                lower = (1.0 - east) * moved[2] + east * moved[3]
                out[field, pl.ds(start, chunk), pl.ds(col, cols), :] = (
                    1.0 - down
                ) * upper + down * lower

    inner_lat, inner_lon = lat_points - 1, lon_points - 1

    @pl.loop(0, inner_lat)
    def _(i):
        row = pl.multiple_of(HALF + i * SPACING, HALF)

        @pl.loop(0, inner_lon)
        def _(j):
            col = pl.multiple_of(HALF + j * SPACING, HALF)
            region(i + 1, j + 1, row, col, SPACING, SPACING, 0, 0)

        region(i + 1, 0, row, 0, SPACING, HALF, 0, HALF)
        region(i + 1, lon_points, row, width - HALF, SPACING, HALF, 0, 0)

    @pl.loop(0, inner_lon)
    def _(j):
        col = pl.multiple_of(HALF + j * SPACING, HALF)
        region(0, j + 1, 0, col, HALF, SPACING, HALF, 0)
        region(lat_points, j + 1, height - HALF, col, HALF, SPACING, 0, 0)

    for i, row, row_shift in ((0, 0, HALF), (lat_points, height - HALF, 0)):
        for j, col, col_shift in ((0, 0, HALF), (lon_points, width - HALF, 0)):
            region(i, j, row, col, HALF, HALF, row_shift, col_shift)


def local(state, field_rate, obs_cell, obs_value, obs_var, obs_count, radius):
    fields, height, width, members = state.shape
    lat_points, lon_points = obs_cell.shape[0], obs_cell.shape[1]
    g = SUBSTEPS
    vmem = pl.BlockSpec(memory_space=pltpu.VMEM)
    anywhere = pl.BlockSpec(memory_space=pl.ANY)
    sides = pltpu.VMEM((fields, 2, height // 2, 2 * g, members), F32)
    copies = 6 * fields + 8
    forecast, weights = pl.pallas_call(
        forecast_kernel,
        out_shape=(
            jax.ShapeDtypeStruct(state.shape, F32),
            jax.ShapeDtypeStruct((lat_points + 2, lon_points + 2, members, members), F32),
        ),
        in_specs=[anywhere] * 7,
        out_specs=(anywhere, vmem),
        scratch_shapes=[
            pltpu.SMEM(field_rate.shape, F32),
            pltpu.SMEM(obs_count.shape, jnp.int32),
            pltpu.SMEM(radius.shape, jnp.int32),
            pltpu.VMEM(obs_cell.shape, jnp.int32),
            pltpu.VMEM(obs_value.shape, F32),
            pltpu.VMEM(obs_var.shape, F32),
            pltpu.VMEM((fields, height + 2 * g, width + 2 * g, members), F32),
            sides,
            sides,
            pltpu.VMEM((lat_points, lon_points, SPACING * SPACING, 2 * members), F32),
            pltpu.VMEM(state.shape, F32),
            pltpu.SemaphoreType.DMA((6,)),
            pltpu.SemaphoreType.DMA((fields,)),
            pltpu.SemaphoreType.DMA((fields,)),
            pltpu.SemaphoreType.DMA((copies,)),
            pltpu.SemaphoreType.DMA((copies,)),
        ],
        compiler_params=pltpu.CompilerParams(
            vmem_limit_bytes=VMEM_BYTES, collective_id=0, has_side_effects=True
        ),
    )(field_rate, obs_count, radius, obs_cell, obs_value, obs_var, state)
    field_block = pl.BlockSpec((1, height, width, members), lambda f: (f, 0, 0, 0))
    return pl.pallas_call(
        analysis_kernel,
        grid=(fields,),
        out_shape=jax.ShapeDtypeStruct(state.shape, F32),
        in_specs=[field_block, vmem],
        out_specs=field_block,
        scratch_shapes=[pltpu.VMEM((2,) + weights.shape, BF16)],
        compiler_params=pltpu.CompilerParams(vmem_limit_bytes=VMEM_BYTES),
    )(forecast, weights)


def solution(mesh):
    in_specs = (
        P(None, "lat", "lon", None),
        P(),
        P("lat", "lon", None),
        P("lat", "lon", None),
        P("lat", "lon", None),
        P("lat", "lon"),
        P("lat", "lon"),
    )
    out_specs = P(None, "lat", "lon", None)
    return jax.shard_map(local, mesh=mesh, in_specs=in_specs, out_specs=out_specs, check_vma=False)
```

```python
import jax
import jax.numpy as jnp
from jax import lax
from jax.experimental import pallas as pl
from jax.experimental.pallas import tpu as pltpu
from jax.sharding import PartitionSpec as P

SPACING = 16
SUBSTEPS = 4
NS_ITERS = 6
HALF = SPACING // 2
VMEM_BYTES = 50 * 1024 * 1024
F32 = jnp.float32
BF16 = jnp.bfloat16


def split(x):
    high = x.astype(BF16)
    return high, (x - high.astype(F32)).astype(BF16)


def product(left, right):
    n = right[0].shape[1]
    row = jnp.concatenate(right, axis=1)
    both = jnp.dot(
        jnp.concatenate(left, axis=1),
        jnp.concatenate([row, row], axis=0),
        preferred_element_type=F32,
    )
    return both[:, :n] + both[:, n:]


def substep(step, field, rate, ext, out):
    rows, cols = ext.shape[1], ext.shape[2]
    own = out.shape[2]
    scale = 0.125 * rate
    first, last = step + 1, rows - 1 - step

    def conductance(u):
        return scale * (3.0 + jnp.tanh(u))

    def body(r, carry):
        u, h, north = carry
        below = ext[field, r + 1]
        h_below = conductance(below)
        south = (h + h_below) * (below - u)
        east = (h + pltpu.roll(h, cols - 1, 0)) * (pltpu.roll(u, cols - 1, 0) - u)
        new = u + ((south - north) + (east - pltpu.roll(east, 1, 0)))
        if step == SUBSTEPS - 1:
            out[field, r - SUBSTEPS] = new[:own]
        else:
            ext[field, r] = new
        return below, h_below, south

    above, u = ext[field, step], ext[field, first]
    h_above, h = conductance(above), conductance(u)
    lax.fori_loop(first, last, body, (u, h, (h_above + h) * (u - above)), unroll=2)


def point_sums(a, b, count, radius, obs_cell, obs_value, obs_var, sums):
    slots = obs_cell.shape[2]
    cells, members = sums.shape[2], sums.shape[3] // 2
    which = lax.broadcasted_iota(jnp.int32, (cells, slots), 0)
    place = lax.broadcasted_iota(jnp.int32, (cells, members), 0)
    centre = 0.5 * SPACING - 0.5
    distance = ((place // SPACING).astype(F32) - centre) ** 2 + (
        (place % SPACING).astype(F32) - centre
    ) ** 2
    slot = lax.broadcasted_iota(jnp.int32, (1, slots), 1)
    one = pl.ds(b, 1)
    chosen = (which == obs_cell[a, one]).astype(F32).astype(BF16)
    weight = jnp.where(slot < count[a, b], 1.0 / obs_var[a, one], 0.0)
    valued = weight * obs_value[a, one]
    both = jnp.concatenate(
        [
            jnp.broadcast_to(weight, (members, slots)),
            jnp.broadcast_to(valued, (members, slots)),
        ],
        axis=0,
    )
    found = sum(
        lax.dot_general(chosen, part, (((1,), (1,)), ((), ())), preferred_element_type=F32)
        for part in split(both)
    )
    reach = radius[a, b]
    reach_sq = jnp.full((cells, members), reach * reach, jnp.int32).astype(F32)
    locality = jnp.maximum(1.0 - distance / reach_sq, 0.0) ** 2
    sums[a, b, :, :members] = found[:, :members] * locality
    sums[a, b, :, members:] = found[:, members:] * locality


def column_weights(columns, forecast, sums, weights):
    lat_points, cells = sums.shape[0], sums.shape[2]
    members = forecast.shape[3]
    points = [(a, b) for b in columns for a in range(lat_points)]
    identity = (
        lax.broadcasted_iota(jnp.int32, (members, members), 0)
        == lax.broadcasted_iota(jnp.int32, (members, members), 1)
    ).astype(F32)
    states = []
    for a, b in points:
        weight_sum = sums[a, b, :, :members]
        value_sum = sums[a, b, :, members:]
        tile = forecast[
            0, a * SPACING : (a + 1) * SPACING, b * SPACING : (b + 1) * SPACING, :
        ]
        tile = tile.reshape(cells, members)
        average = jnp.mean(tile, axis=1, keepdims=True)
        departure = tile - average
        scaled = split(weight_sum * departure)
        forced = split(value_sum - average * weight_sum)
        quads = lax.dot_general(
            jnp.concatenate(split(departure), axis=1),
            jnp.concatenate(scaled + forced, axis=1),
            (((0,), (0,)), ((), ())),
            preferred_element_type=F32,
        )
        quads = quads[:members] + quads[members:]
        gram = quads[:, :members] + quads[:, members : 2 * members]
        forcing = quads[:, 2 * members : 3 * members] + quads[:, 3 * members :]
        system = (members - 1.0) * identity + gram
        norm = jnp.sqrt(jnp.sum(system * system, keepdims=True) + 1e-06)
        states.append((system / norm, forcing, norm))
    iterates = [split(s[0]) for s in states]
    middles = [split(1.5 * identity - 0.5 * s[0]) for s in states]
    iterates = [split(product(x, m)) for x, m in zip(iterates, middles)]
    inverses = middles
    for repeat in range(1, NS_ITERS):
        middles = [
            split(1.5 * identity - 0.5 * product(z, y)) for z, y in zip(inverses, iterates)
        ]
        if repeat < NS_ITERS - 1:
            iterates = [split(product(y, m)) for y, m in zip(iterates, middles)]
        raw = [product(m, z) for m, z in zip(middles, inverses)]
        inverses = [split(z) for z in raw]
    for n, (a, b) in enumerate(points):
        forcing, norm = states[n][1], states[n][2]
        pulled = product(inverses[n], split(product(inverses[n], split(forcing))))
        moved = (members - 1.0) ** 0.5 / jnp.sqrt(norm) * raw[n] + pulled / norm
        weights[a + 1, b + 1] = moved + (1.0 / members - jnp.mean(moved, axis=0, keepdims=True))


def forecast_kernel(
    rate_in, count_in, radius_in, cell_in, value_in, var_in, state,
    forecast_out, weights,
    rate, count, radius, obs_cell, obs_value, obs_var,
    ext, packed, got, sums, forecast, small_sem, load_sem, store_sem, send_sem, recv_sem,
):
    fields, height, width = state.shape[0], state.shape[1], state.shape[2]
    lat_points, lon_points = sums.shape[0], sums.shape[1]
    g = SUBSTEPS
    end = g + height
    half = height // 2
    lon, lat = lax.axis_index("lon"), lax.axis_index("lat")
    lon_size, lat_size = lax.axis_size("lon"), lax.axis_size("lat")
    has_north, has_south = lat > 0, lat < lat_size - 1
    to_east = {"lon": lax.rem(lon + 1, lon_size)}
    to_west = {"lon": lax.rem(lon + lon_size - 1, lon_size)}
    to_north = {"lat": lax.rem(lat + lat_size - 1, lat_size)}
    to_south = {"lat": lax.rem(lat + 1, lat_size)}
    mesh_ids = pl.DeviceIdType.MESH

    barrier = pltpu.get_barrier_semaphore()
    pl.semaphore_signal(barrier, inc=1, device_id=to_east, device_id_type=mesh_ids)
    pl.semaphore_signal(barrier, inc=1, device_id=to_west, device_id_type=mesh_ids)

    @pl.when(has_north)
    def _():
        pl.semaphore_signal(barrier, inc=1, device_id=to_north, device_id_type=mesh_ids)

    @pl.when(has_south)
    def _():
        pl.semaphore_signal(barrier, inc=1, device_id=to_south, device_id_type=mesh_ids)

    loads = [
        pltpu.make_async_copy(state.at[f], ext.at[f, g:end, :width], load_sem.at[f])
        for f in range(fields)
    ]
    small = [
        pltpu.make_async_copy(src, dst, small_sem.at[n])
        for n, (src, dst) in enumerate(
            (
                (rate_in, rate),
                (count_in, count),
                (radius_in, radius),
                (cell_in, obs_cell),
                (value_in, obs_value),
                (var_in, obs_var),
            )
        )
    ]
    for load in loads + small:
        load.start()
    north_peers = lax.div(lat + lat_size - 1, lat_size)
    south_peers = lax.div(2 * lat_size - 2 - lat, lat_size)
    pl.semaphore_wait(barrier, 2 + north_peers + south_peers)

    def remote(k, src, dst, target):
        return pltpu.make_async_remote_copy(
            src_ref=src, dst_ref=dst, send_sem=send_sem.at[k], recv_sem=recv_sem.at[k],
            device_id=target, device_id_type=mesh_ids,
        )

    def start_lat(north, south):
        @pl.when(has_north)
        def _():
            for copy in north:
                copy.start()

        @pl.when(has_south)
        def _():
            for copy in south:
                copy.start()

    def wait_lat(north, south):
        @pl.when(has_north)
        def _():
            for copy in north:
                copy.wait_send()
            for copy in south:
                copy.wait_recv()

        @pl.when(has_south)
        def _():
            for copy in south:
                copy.wait_send()
            for copy in north:
                copy.wait_recv()

    eastward, westward, northward, southward, corner_n, corner_s = [], [], [], [], [], []
    for f in range(fields):
        k = 6 * f
        eastward.append(remote(k, packed.at[f, 1], got.at[f, 1], to_east))
        westward.append(remote(k + 1, packed.at[f, 0], got.at[f, 0], to_west))
        northward.append(remote(k + 2, state.at[f, :g], ext.at[f, end:, :width], to_north))
        southward.append(
            remote(k + 3, state.at[f, height - g :], ext.at[f, :g, :width], to_south)
        )
        corner_n.append(
            remote(k + 4, ext.at[f, g : 2 * g, width:], ext.at[f, end:, width:], to_north)
        )
        corner_s.append(
            remote(k + 5, ext.at[f, height:end, width:], ext.at[f, :g, width:], to_south)
        )

    def send_ghosts(f):
        for side, cols, part in (
            (1, slice(width - 2 * g, width), slice(g, None)),
            (0, slice(0, 2 * g), slice(0, g)),
        ):
            upper = ext[f, g : g + half, cols][:, part]
            lower = ext[f, g + half : end, cols][:, part]
            packed[f, side] = jnp.concatenate([upper, lower], axis=1)
            (westward, eastward)[side][f].start()
        start_lat([northward[f]], [southward[f]])

    def place_sides(f):
        eastward[f].wait()
        westward[f].wait()
        east, west = got[f, 0], got[f, 1]
        ext[f, g : g + half, width:] = jnp.concatenate([east[:, :g], west[:, :g]], axis=1)
        ext[f, g + half : end, width:] = jnp.concatenate([east[:, g:], west[:, g:]], axis=1)
        start_lat([corner_n[f]], [corner_s[f]])

    def finish_ghosts(f):
        wait_lat([northward[f], corner_n[f]], [southward[f], corner_s[f]])

        @pl.when(jnp.logical_not(has_north))
        def _():
            for r in range(g):
                ext[f, r] = ext[f, 2 * g - 1 - r]

        @pl.when(jnp.logical_not(has_south))
        def _():
            for r in range(g):
                ext[f, end + r] = ext[f, end - 1 - r]

    for f in range(fields):
        loads[f].wait()
        if f == 0:
            send_ghosts(f)

    for load in small:
        load.wait()

    @pl.loop(0, lat_points)
    def _(a):
        @pl.loop(0, lon_points)
        def _(b):
            point_sums(a, b, count, radius, obs_cell, obs_value, obs_var, sums)

    stores = [
        pltpu.make_async_copy(forecast.at[f], forecast_out.at[f], store_sem.at[f])
        for f in range(fields)
    ]
    place_sides(0)
    for f in range(1, fields):
        send_ghosts(f)
    finish_ghosts(0)
    for step in range(SUBSTEPS):
        substep(step, 0, rate[0], ext, forecast)
    stores[0].start()

    k = 6 * fields
    lat_rows, lon_cols = pl.ds(1, lat_points), pl.ds(1, lon_points)
    w_east = remote(k, weights.at[lat_rows, lon_points], weights.at[lat_rows, 0], to_east)
    w_west = remote(
        k + 1, weights.at[lat_rows, 1], weights.at[lat_rows, lon_points + 1], to_west
    )
    w_north = [remote(k + 2, weights.at[1, lon_cols], weights.at[lat_points + 1, lon_cols], to_north)]
    w_south = [remote(k + 3, weights.at[lat_points, lon_cols], weights.at[0, lon_cols], to_south)]
    c_north, c_south = [], []
    for n, b in enumerate((0, lon_points + 1)):
        c_north.append(
            remote(k + 4 + n, weights.at[1, b], weights.at[lat_points + 1, b], to_north)
        )
        c_south.append(remote(k + 6 + n, weights.at[lat_points, b], weights.at[0, b], to_south))

    column_weights((0, lon_points - 1), forecast, sums, weights)

    w_east.start()
    w_west.start()
    for f in range(1, fields):
        place_sides(f)

    for b in range(1, lon_points - 1, 2):
        column_weights(range(b, min(b + 2, lon_points - 1)), forecast, sums, weights)

    start_lat(w_north, w_south)
    for f in range(1, fields):
        finish_ghosts(f)
        for step in range(SUBSTEPS):
            substep(step, f, rate[f], ext, forecast)
            if f == fields - 1 and step == SUBSTEPS - 2:
                w_east.wait()
                w_west.wait()
                start_lat(c_north, c_south)
        stores[f].start()
    wait_lat(w_north + c_north, w_south + c_south)

    @pl.when(jnp.logical_not(has_north))
    def _():
        weights[0] = weights[1]

    @pl.when(jnp.logical_not(has_south))
    def _():
        weights[lat_points + 1] = weights[lat_points]

    for store in stores:
        store.wait()


def analysis_kernel(forecast, weights, out, parts):
    fields, height, width, members = forecast.shape
    lat_points, lon_points = height // SPACING, width // SPACING

    @pl.when(pl.program_id(0) == 0)
    def _():
        @pl.loop(0, lat_points + 2)
        def _(i):
            for j in range(lon_points + 2):
                parts[0, i, j], parts[1, i, j] = split(weights[i, j])

    def region(i, j, row, col, rows, cols, row_shift, col_shift):
        corners = ((0, 0), (0, 1), (1, 0), (1, 1))
        high, low = (
            jnp.concatenate([parts[n, i + di, j + dj] for di, dj in corners], axis=1)
            for n in range(2)
        )
        right = jnp.concatenate([high, high, low], axis=0)
        across = lax.broadcasted_iota(jnp.int32, (cols, members), 0) + col_shift
        east = (across.astype(F32) + 0.5) * (1.0 / SPACING)
        own = 1.0 - east
        for field in range(fields):
            cells = forecast[field, pl.ds(row, rows), pl.ds(col, cols), :]
            left = split(cells.reshape(rows * cols, members))
            moved = jnp.dot(
                jnp.concatenate(left + left[:1], axis=1), right, preferred_element_type=F32
            )
            for r in range(rows):
                down = (row_shift + r + 0.5) / SPACING
                line = moved[r * cols : (r + 1) * cols]
                quarters = [line[:, k * members : (k + 1) * members] for k in range(4)]
                upper = own * quarters[0] + east * quarters[1]
                lower = own * quarters[2] + east * quarters[3]
                out[field, row + r, pl.ds(col, cols), :] = (1.0 - down) * upper + down * lower

    inner_lat, inner_lon = lat_points - 1, lon_points - 1

    @pl.loop(0, inner_lat)
    def _(i):
        row = pl.multiple_of(HALF + i * SPACING, HALF)

        @pl.loop(0, inner_lon)
        def _(j):
            col = pl.multiple_of(HALF + j * SPACING, HALF)
            region(i + 1, j + 1, row, col, SPACING, SPACING, 0, 0)

        region(i + 1, 0, row, 0, SPACING, HALF, 0, HALF)
        region(i + 1, lon_points, row, width - HALF, SPACING, HALF, 0, 0)

    @pl.loop(0, inner_lon)
    def _(j):
        col = pl.multiple_of(HALF + j * SPACING, HALF)
        region(0, j + 1, 0, col, HALF, SPACING, HALF, 0)
        region(lat_points, j + 1, height - HALF, col, HALF, SPACING, 0, 0)

    for i, row, row_shift in ((0, 0, HALF), (lat_points, height - HALF, 0)):
        for j, col, col_shift in ((0, 0, HALF), (lon_points, width - HALF, 0)):
            region(i, j, row, col, HALF, HALF, row_shift, col_shift)


def local(state, field_rate, obs_cell, obs_value, obs_var, obs_count, radius):
    fields, height, width, members = state.shape
    lat_points, lon_points = obs_cell.shape[0], obs_cell.shape[1]
    g = SUBSTEPS
    vmem = pl.BlockSpec(memory_space=pltpu.VMEM)
    hbm = pl.BlockSpec(memory_space=pltpu.HBM)
    sides = pltpu.VMEM((fields, 2, height // 2, 2 * g, members), F32)
    copies = 6 * fields + 8
    forecast, weights = pl.pallas_call(
        forecast_kernel,
        out_shape=(
            jax.ShapeDtypeStruct(state.shape, F32),
            jax.ShapeDtypeStruct((lat_points + 2, lon_points + 2, members, members), F32),
        ),
        in_specs=[hbm] * 7,
        out_specs=(hbm, vmem),
        scratch_shapes=[
            pltpu.SMEM(field_rate.shape, F32),
            pltpu.SMEM(obs_count.shape, jnp.int32),
            pltpu.SMEM(radius.shape, jnp.int32),
            pltpu.VMEM(obs_cell.shape, jnp.int32),
            pltpu.VMEM(obs_value.shape, F32),
            pltpu.VMEM(obs_var.shape, F32),
            pltpu.VMEM((fields, height + 2 * g, width + 2 * g, members), F32),
            sides,
            sides,
            pltpu.VMEM((lat_points, lon_points, SPACING * SPACING, 2 * members), F32),
            pltpu.VMEM(state.shape, F32),
            pltpu.SemaphoreType.DMA((6,)),
            pltpu.SemaphoreType.DMA((fields,)),
            pltpu.SemaphoreType.DMA((fields,)),
            pltpu.SemaphoreType.DMA((copies,)),
            pltpu.SemaphoreType.DMA((copies,)),
        ],
        compiler_params=pltpu.CompilerParams(
            vmem_limit_bytes=VMEM_BYTES, collective_id=0, has_side_effects=True
        ),
    )(field_rate, obs_count, radius, obs_cell, obs_value, obs_var, state)
    field_block = pl.BlockSpec((1, height, width, members), lambda f: (f, 0, 0, 0))
    return pl.pallas_call(
        analysis_kernel,
        grid=(fields,),
        out_shape=jax.ShapeDtypeStruct(state.shape, F32),
        in_specs=[field_block, vmem],
        out_specs=field_block,
        scratch_shapes=[pltpu.VMEM((2,) + weights.shape, BF16)],
        compiler_params=pltpu.CompilerParams(vmem_limit_bytes=VMEM_BYTES),
    )(forecast, weights)


def solution(mesh):
    in_specs = (
        P(None, "lat", "lon", None),
        P(),
        P("lat", "lon", None),
        P("lat", "lon", None),
        P("lat", "lon", None),
        P("lat", "lon"),
        P("lat", "lon"),
    )
    out_specs = P(None, "lat", "lon", None)
    return jax.shard_map(local, mesh=mesh, in_specs=in_specs, out_specs=out_specs, check_vma=False)
```
